32 devices in a mesh: row: 4 (over x, core), col: 8 (over z, y).
Axes of the slice: x: 2, y: 2, z: 4, core: 2. Of those that a mesh axis runs over, the one named last changes fastest.
Arguments:
- t_slab: bfloat16 [4, 2, 512, 64], P('row', None, 'col'), may hold values from -6 to 6
- w_cycle: bfloat16 [128, 16384], P('row', 'col'), may hold values from -0.5 to 0.5
Outputs:
- t_amp: bfloat16 [2048, 128], P('row', 'col')
- cycle_z: float32 [2048, 16384], P('row', 'col')
The draws below stay inside these ranges and needn't reach their ends.
All inputs are finite; a program needn't handle non-finite values.
Results may differ from the reference program's by a relative error of at most 0.001.
Values may be sent and summed in bfloat16 or wider, within the bound.
A program may use at most 64 MiB of HBM per device.

```python
import jax
import jax.numpy as jnp

VIRT = 512
PANELS = 2
PANEL_WIDTH = 64
OCC = 4
KC = 128
JB = 16384


def shard_levels(stream_key, extent, shards, smallest, largest):
    def one(position, blocks):
        steps = jax.random.uniform(jax.random.fold_in(jax.random.fold_in(stream_key, 6), position), (blocks,), jnp.float32, smallest / len(shards), largest / len(shards))
        return jnp.repeat(jnp.exp(steps), extent[position] // blocks).reshape((-1,) + (1,) * (len(extent) - position - 1))

    factor_of = one(*shards[0])
    for cut in shards[1:]:
        factor_of = factor_of * one(*cut)
    return factor_of


def normal_values(own_key, extent, spread, limit, pieces=(), dtype=jnp.bfloat16):
    factor_of = shard_levels(own_key, extent, pieces, -0.22, 0.18) if pieces else 1.0
    array = jax.random.normal(own_key, extent, jnp.float32) * spread * factor_of
    return jnp.minimum(jnp.maximum(array, -limit), limit).astype(dtype)


def setup_inputs(seed: int = 0) -> dict:
    keys = jax.random.split(jax.random.key(seed), 3)
    return {
        "t_slab": normal_values(keys[0], (OCC, PANELS, VIRT, PANEL_WIDTH), 1.0, 6.0, ((0, 4), (2, 8))),
        "w_cycle": normal_values(keys[1], (KC, JB), KC ** -0.5, 0.5, ((0, 4), (1, 8))),
    }


def reference(t_slab, w_cycle):
    regrouped = jnp.transpose(t_slab, (0, 2, 1, 3)).reshape(OCC * VIRT, PANELS * PANEL_WIDTH)
    cycle_z = jnp.dot(regrouped, w_cycle, preferred_element_type=jnp.float32)
    return regrouped, cycle_z
```

```python
import functools

import jax
import jax.numpy as jnp
from jax import lax
from jax.experimental import pallas as pl
from jax.experimental.pallas import tpu as pltpu
from jax.sharding import PartitionSpec as P

PIECES = 4
TILE = 256
CORES = 2


def gather_kernel(
    n_row, n_col, pieces, t_ref, w_ref, t_all, w_all, t_own, local_sem,
    w_chip_send, w_chip_recv, w_core_send, w_core_recv,
    t_z_send, t_z_recv, t_y_send, t_y_recv,
):
    row, col = lax.axis_index("row"), lax.axis_index("col")
    chips, core = n_row // CORES, lax.rem(row, CORES)
    chip = row // CORES
    levels, side = n_col // 2, lax.rem(col, 2)
    level = col // 2
    width = w_ref.shape[1] // pieces

    def chip_peer(k):
        return lax.rem(chip + k, chips) * CORES + core

    def level_peer(k):
        return lax.rem(level + k, levels) * 2 + side

    other_core = chip * CORES + 1 - core
    other_side = level * 2 + 1 - side

    barrier = pltpu.get_barrier_semaphore()
    peers = [{"row": chip_peer(k), "col": col} for k in range(1, chips)]
    peers.append({"row": other_core, "col": col})
    peers += [{"row": row, "col": level_peer(k)} for k in range(1, levels)]
    peers.append({"row": row, "col": other_side})
    for peer in peers:
        pl.semaphore_signal(barrier, inc=1, device_id=peer)

    t_in = pltpu.make_async_copy(t_ref, t_own, local_sem.at[0])
    t_in.start()
    w_in = pltpu.make_async_copy(w_ref, w_all.at[row], local_sem.at[1])
    w_in.start()
    t_in.wait()
    t_all[col] = jnp.concatenate(
        [t_own[0, k] for k in range(t_own.shape[1])], axis=1
    )
    pl.semaphore_wait(barrier, len(peers))

    def w_chip(k, j):
        columns = pl.ds(j * width, width)
        return pltpu.make_async_remote_copy(
            src_ref=w_ref.at[:, columns],
            dst_ref=w_all.at[row, :, columns],
            send_sem=w_chip_send.at[k, j],
            recv_sem=w_chip_recv.at[k, j],
            device_id={"row": chip_peer(k), "col": col},
        )

    def w_core(k, j):
        columns = pl.ds(j * width, width)
        slot = lax.rem(chip - k + chips, chips) * CORES + core
        source = w_ref if k == 0 else w_all.at[slot]
        return pltpu.make_async_remote_copy(
            src_ref=source.at[:, columns],
            dst_ref=w_all.at[slot, :, columns],
            send_sem=w_core_send.at[k, j],
            recv_sem=w_core_recv.at[k, j],
            device_id={"row": other_core, "col": col},
        )

    def t_z(k):
        return pltpu.make_async_remote_copy(
            src_ref=t_all.at[col],
            dst_ref=t_all.at[col],
            send_sem=t_z_send.at[k],
            recv_sem=t_z_recv.at[k],
            device_id={"row": row, "col": level_peer(k)},
        )

    def t_y(k):
        slot = lax.rem(level - k + levels, levels) * 2 + side
        return pltpu.make_async_remote_copy(
            src_ref=t_all.at[slot],
            dst_ref=t_all.at[slot],
            send_sem=t_y_send.at[k],
            recv_sem=t_y_recv.at[k],
            device_id={"row": row, "col": other_side},
        )

    w_out = [(k, j) for j in range(pieces) for k in range(1, chips)]
    t_out = list(range(1, levels))
    for k, j in w_out:
        w_chip(k, j).start()
    for k in t_out:
        t_z(k).start()
    t_y(0).start()
    for j in range(pieces):
        w_core(0, j).start()

    for step in range(max(len(w_out), len(t_out))):
        if step < len(w_out):
            w_chip(*w_out[step]).wait_recv()
            w_core(*w_out[step]).start()
        if step < len(t_out):
            t_z(t_out[step]).wait_recv()
            t_y(t_out[step]).start()

    w_in.wait()
    for k in range(levels):
        t_y(k).wait_recv()
    for k in range(chips):
        for j in range(pieces):
            w_core(k, j).wait_recv()
    for k, j in w_out:
        w_chip(k, j).wait_send()
    for k in t_out:
        t_z(k).wait_send()
    for k in range(levels):
        t_y(k).wait_send()
    for k in range(chips):
        for j in range(pieces):
            w_core(k, j).wait_send()


def product_kernel(t_ref, w_ref, amp_ref, z_ref, z_tiles, turned, amp_own, sems, amp_sem):
    col = lax.axis_index("col")
    tile = z_tiles.shape[2]
    kc = t_ref.shape[2]
    t_full = t_ref[...].reshape(-1, kc)
    copies = []
    for j in range(z_tiles.shape[0]):
        columns = pl.ds(j * tile, tile)
        z_tiles[j] = jnp.dot(
            t_full,
            w_ref[:, :, columns].reshape(kc, tile),
            preferred_element_type=jnp.float32,
        )
        copy = pltpu.make_async_copy(
            z_tiles.at[j], z_ref.at[:, columns], sems.at[j]
        )
        copy.start()
        copies.append(copy)
    turned[...] = t_full.astype(jnp.float32).T.reshape(turned.shape)
    amp_own[...] = turned[col].astype(amp_own.dtype)
    copy = pltpu.make_async_copy(amp_own, amp_ref, amp_sem)
    copy.start()
    copies.append(copy)
    for copy in copies:
        copy.wait()


def shards(n_row, n_col, t_slab, w_cycle):
    _, panels, share, panel_width = t_slab.shape
    depth, jb = w_cycle.shape
    kc = panels * panel_width
    chips, levels = n_row // CORES, n_col // 2
    anywhere = pl.BlockSpec(memory_space=pl.ANY)
    vmem = pl.BlockSpec(memory_space=pltpu.VMEM)
    dma = pltpu.SemaphoreType.DMA
    t_all, w_all = pl.pallas_call(
        functools.partial(gather_kernel, n_row, n_col, PIECES),
        out_shape=(
            pltpu.VMEM((n_col, share, kc), t_slab.dtype),
            pltpu.VMEM((n_row, depth, jb), w_cycle.dtype),
        ),
        in_specs=[anywhere] * 2,
        out_specs=(vmem, vmem),
        scratch_shapes=[
            pltpu.VMEM(t_slab.shape, t_slab.dtype),
            dma((2,)),
            dma((chips, PIECES)), dma((chips, PIECES)),
            dma((chips, PIECES)), dma((chips, PIECES)),
            dma((levels,)), dma((levels,)),
            dma((levels,)), dma((levels,)),
        ],
        compiler_params=pltpu.CompilerParams(
            collective_id=0, has_side_effects=True
        ),
        name="gather",
    )(t_slab, w_cycle)
    rows = n_col * share
    amp, z = pl.pallas_call(
        product_kernel,
        out_shape=(
            jax.ShapeDtypeStruct((kc // n_col, rows), t_slab.dtype),
            jax.ShapeDtypeStruct((rows, jb), jnp.float32),
        ),
        in_specs=[vmem] * 2,
        out_specs=(anywhere, anywhere),
        scratch_shapes=[
            pltpu.VMEM((jb // TILE, rows, TILE), jnp.float32),
            pltpu.VMEM((n_col, kc // n_col, rows), jnp.float32),
            pltpu.VMEM((kc // n_col, rows), t_slab.dtype),
            dma((jb // TILE,)),
            dma,
        ],
        compiler_params=pltpu.CompilerParams(vmem_limit_bytes=32 * 2**20),
        name="product",
    )(t_all, w_all)
    return amp.T, z


def solution(mesh):
    placed = (P("row", None, "col", None), P("row", "col"))
    return jax.shard_map(
        functools.partial(shards, mesh.shape["row"], mesh.shape["col"]),
        mesh=mesh,
        in_specs=placed,
        out_specs=(P("row", "col"), P("row", "col")),
        check_vma=False,
    )
```

```python
import functools

import jax
import jax.numpy as jnp
from jax import lax
from jax.experimental import pallas as pl
from jax.experimental.pallas import tpu as pltpu
from jax.sharding import PartitionSpec as P

PIECES = 2
DIRECT = 1
TILE = 256
CORES = 2


def gather_kernel(
    n_row, n_col, t_ref, w_ref, t_all, w_all, t_in, local_sem,
    chip_send, chip_recv, core_send, core_recv, twin_send, twin_recv, t_send, t_recv,
):
    row, col = lax.axis_index("row"), lax.axis_index("col")
    chips, core = n_row // CORES, lax.rem(row, CORES)
    chip = row // CORES
    pieces = chip_send.shape[1]
    kc = t_all.shape[2]
    width = w_ref.shape[1] // pieces
    relayed = pieces - DIRECT

    barrier = pltpu.get_barrier_semaphore()
    for k in range(1, n_row):
        pl.semaphore_signal(
            barrier, inc=1, device_id={"row": lax.rem(row + k, n_row), "col": col}
        )
    for k in range(1, n_col):
        pl.semaphore_signal(
            barrier, inc=1, device_id={"row": row, "col": lax.rem(col + k, n_col)}
        )
    t_stage = pltpu.make_async_copy(t_ref, t_in, local_sem.at[0])
    t_stage.start()
    w_stage = pltpu.make_async_copy(w_ref, w_all.at[row], local_sem.at[1])
    w_stage.start()

    def chip_at(k):
        return lax.rem(chip + k + chips, chips)

    def columns(j):
        return pl.ds(j * width, width)

    def to_chip(k, j):
        return pltpu.make_async_remote_copy(
            src_ref=w_ref.at[:, columns(j)],
            dst_ref=w_all.at[row, :, columns(j)],
            send_sem=chip_send.at[k, j],
            recv_sem=chip_recv.at[k, j],
            device_id={"row": chip_at(k) * CORES + core, "col": col},
        )

    def to_twin(k, j):
        return pltpu.make_async_remote_copy(
            src_ref=w_ref.at[:, columns(j)],
            dst_ref=w_all.at[row, :, columns(j)],
            send_sem=twin_send.at[k, j - relayed],
            recv_sem=twin_recv.at[k, j - relayed],
            device_id={"row": chip_at(k) * CORES + 1 - core, "col": col},
        )

    def to_core(k, j):
        slot = chip_at(-k) * CORES + core
        source = w_ref if k == 0 else w_all.at[slot]
        return pltpu.make_async_remote_copy(
            src_ref=source.at[:, columns(j)],
            dst_ref=w_all.at[slot, :, columns(j)],
            send_sem=core_send.at[k, j],
            recv_sem=core_recv.at[k, j],
            device_id={"row": chip * CORES + 1 - core, "col": col},
        )

    def t_to(k):
        return pltpu.make_async_remote_copy(
            src_ref=t_all.at[col],
            dst_ref=t_all.at[col],
            send_sem=t_send.at[k],
            recv_sem=t_recv.at[k],
            device_id={"row": row, "col": lax.rem(col + k, n_col)},
        )

    others = range(1, chips)
    pl.semaphore_wait(barrier, n_row + n_col - 2)
    for j in range(pieces):
        for k in others:
            to_chip(k, j).start()
            if j >= relayed:
                to_twin(k, j).start()
    t_stage.wait()
    t_all[col] = jnp.concatenate(
        [t_in[0, k] for k in range(t_in.shape[1])], axis=1
    )
    for k in range(1, n_col):
        t_to(k).start()
    for j in range(pieces):
        to_core(0, j).start()

    for j in range(relayed):
        for k in others:
            to_chip(k, j).wait_recv()
            to_core(k, j).start()
    w_stage.wait()
    for k in range(1, n_col):
        t_to(k).wait_recv()
    for j in range(pieces):
        to_core(0, j).wait_recv()
        for k in others:
            if j < relayed:
                to_core(k, j).wait_recv()
            else:
                to_chip(k, j).wait_recv()
                to_twin(k, j).wait_recv()

    for k in range(1, n_col):
        t_to(k).wait_send()
    for j in range(pieces):
        to_core(0, j).wait_send()
        for k in others:
            to_chip(k, j).wait_send()
            if j < relayed:
                to_core(k, j).wait_send()
            else:
                to_twin(k, j).wait_send()


def product_kernel(t_ref, w_ref, amp_ref, z_ref, z_tiles, turned, amp_own, sems, amp_sem):
    col = lax.axis_index("col")
    tile = z_tiles.shape[2]
    kc = t_ref.shape[2]
    t_full = t_ref[...].reshape(-1, kc)
    copies = []
    for j in range(z_tiles.shape[0]):
        columns = pl.ds(j * tile, tile)
        z_tiles[j] = jnp.dot(
            t_full,
            w_ref[:, :, columns].reshape(kc, tile),
            preferred_element_type=jnp.float32,
        )
        copy = pltpu.make_async_copy(
            z_tiles.at[j], z_ref.at[:, columns], sems.at[j]
        )
        copy.start()
        copies.append(copy)
    turned[...] = t_full.astype(jnp.float32).T.reshape(turned.shape)
    amp_own[...] = turned[col].astype(amp_own.dtype)
    copy = pltpu.make_async_copy(amp_own, amp_ref, amp_sem)
    copy.start()
    copies.append(copy)
    for copy in copies:
        copy.wait()


def shards(n_row, n_col, t_slab, w_cycle):
    _, panels, share, panel_width = t_slab.shape
    depth, jb = w_cycle.shape
    kc, rows, chips = panels * panel_width, n_col * share, n_row // CORES
    hbm = pl.BlockSpec(memory_space=pltpu.HBM)
    vmem = pl.BlockSpec(memory_space=pltpu.VMEM)
    dma = pltpu.SemaphoreType.DMA
    t_all, w_all = pl.pallas_call(
        functools.partial(gather_kernel, n_row, n_col),
        out_shape=(
            pltpu.VMEM((n_col, share, kc), t_slab.dtype),
            pltpu.VMEM((n_row, depth, jb), w_cycle.dtype),
        ),
        in_specs=[hbm] * 2,
        out_specs=(vmem, vmem),
        scratch_shapes=[
            pltpu.VMEM(t_slab.shape, t_slab.dtype),
            dma((2,)),
            dma((chips, PIECES)), dma((chips, PIECES)),
            dma((chips, PIECES)), dma((chips, PIECES)),
            dma((chips, max(DIRECT, 1))), dma((chips, max(DIRECT, 1))),
            dma((n_col,)), dma((n_col,)),
        ],
        compiler_params=pltpu.CompilerParams(
            collective_id=0, has_side_effects=True
        ),
        name="gather",
    )(t_slab, w_cycle)
    amp, z = pl.pallas_call(
        product_kernel,
        out_shape=(
            jax.ShapeDtypeStruct((kc // n_col, rows), t_slab.dtype),
            jax.ShapeDtypeStruct((rows, jb), jnp.float32),
        ),
        in_specs=[vmem] * 2,
        out_specs=(hbm, hbm),
        scratch_shapes=[
            pltpu.VMEM((jb // TILE, rows, TILE), jnp.float32),
            pltpu.VMEM((n_col, kc // n_col, rows), jnp.float32),
            pltpu.VMEM((kc // n_col, rows), t_slab.dtype),
            dma((jb // TILE,)),
            dma,
        ],
        compiler_params=pltpu.CompilerParams(vmem_limit_bytes=32 * 2**20),
        name="product",
    )(t_all, w_all)
    return amp.T, z


def solution(mesh):
    placed = (P("row", None, "col", None), P("row", "col"))
    return jax.shard_map(
        functools.partial(shards, mesh.shape["row"], mesh.shape["col"]),
        mesh=mesh,
        in_specs=placed,
        out_specs=(P("row", "col"), P("row", "col")),
        check_vma=False,
    )
```

```python
import functools

import jax
import jax.numpy as jnp
from jax import lax
from jax.experimental import pallas as pl
from jax.experimental.pallas import tpu as pltpu
from jax.sharding import PartitionSpec as P

CUTS = (0, 5, 8)
PIECES = len(CUTS) - 1
TILE = 256
CORES = 2


def gather_kernel(
    n_row, n_col, t_ref, w_ref, t_all, w_all, t_in, local_sem,
    chip_send, chip_recv, core_send, core_recv, t_send, t_recv,
):
    row, col = lax.axis_index("row"), lax.axis_index("col")
    chips, core = n_row // CORES, lax.rem(row, CORES)
    chip = row // CORES
    pieces = chip_send.shape[1]
    kc = t_all.shape[2]
    unit = w_ref.shape[1] // CUTS[-1]

    barrier = pltpu.get_barrier_semaphore()
    for k in range(1, chips):
        pl.semaphore_signal(
            barrier, inc=1,
            device_id={"row": lax.rem(row + k * CORES, n_row), "col": col},
        )
    pl.semaphore_signal(
        barrier, inc=1, device_id={"row": chip * CORES + 1 - core, "col": col}
    )
    for k in range(1, n_col):
        pl.semaphore_signal(
            barrier, inc=1, device_id={"row": row, "col": lax.rem(col + k, n_col)}
        )
    t_stage = pltpu.make_async_copy(t_ref, t_in, local_sem.at[0])
    t_stage.start()
    w_stage = pltpu.make_async_copy(w_ref, w_all.at[row], local_sem.at[1])
    w_stage.start()

    def chip_at(k):
        return lax.rem(chip + k + chips, chips)

    def columns(j):
        return pl.ds(CUTS[j] * unit, (CUTS[j + 1] - CUTS[j]) * unit)

    def to_chip(k, j):
        return pltpu.make_async_remote_copy(
            src_ref=w_all.at[row, :, columns(j)],
            dst_ref=w_all.at[row, :, columns(j)],
            send_sem=chip_send.at[k, j],
            recv_sem=chip_recv.at[k, j],
            device_id={"row": chip_at(k) * CORES + core, "col": col},
        )

    def to_core(k, j):
        slot = chip_at(-k) * CORES + core
        return pltpu.make_async_remote_copy(
            src_ref=w_all.at[slot, :, columns(j)],
            dst_ref=w_all.at[slot, :, columns(j)],
            send_sem=core_send.at[k, j],
            recv_sem=core_recv.at[k, j],
            device_id={"row": chip * CORES + 1 - core, "col": col},
        )

    def t_to(k):
        return pltpu.make_async_remote_copy(
            src_ref=t_all.at[col],
            dst_ref=t_all.at[col],
            send_sem=t_send.at[k],
            recv_sem=t_recv.at[k],
            device_id={"row": row, "col": lax.rem(col + k, n_col)},
        )

    others = range(1, chips)
    pl.semaphore_wait(barrier, chips + n_col - 1)
    w_stage.wait()
    for j in range(pieces):
        to_core(0, j).start()
    for j in range(pieces):
        for k in others:
            to_chip(k, j).start()
    t_stage.wait()
    t_all[col] = jnp.concatenate(
        [t_in[0, k] for k in range(t_in.shape[1])], axis=1
    )
    for k in range(1, n_col):
        t_to(k).start()

    for j in range(pieces):
        for k in others:
            to_chip(k, j).wait_recv()
            to_core(k, j).start()
    for k in range(1, n_col):
        t_to(k).wait_recv()
    for j in range(pieces):
        to_core(0, j).wait_recv()
        for k in others:
            to_core(k, j).wait_recv()

    for k in range(1, n_col):
        t_to(k).wait_send()
    for j in range(pieces):
        to_core(0, j).wait_send()
        for k in others:
            to_chip(k, j).wait_send()
            to_core(k, j).wait_send()


def product_kernel(t_ref, w_ref, amp_ref, z_ref, z_tiles, turned, amp_own, sems, amp_sem):
    col = lax.axis_index("col")
    tile = z_tiles.shape[2]
    kc = t_ref.shape[2]
    t_full = t_ref[...].reshape(-1, kc)
    copies = []
    for j in range(z_tiles.shape[0]):
        columns = pl.ds(j * tile, tile)
        z_tiles[j] = jnp.dot(
            t_full,
            w_ref[:, :, columns].reshape(kc, tile),
            preferred_element_type=jnp.float32,
        )
        copy = pltpu.make_async_copy(
            z_tiles.at[j], z_ref.at[:, columns], sems.at[j]
        )
        copy.start()
        copies.append(copy)
    turned[...] = t_full.astype(jnp.float32).T.reshape(turned.shape)
    amp_own[...] = turned[col].astype(amp_own.dtype)
    copy = pltpu.make_async_copy(amp_own, amp_ref, amp_sem)
    copy.start()
    copies.append(copy)
    for copy in copies:
        copy.wait()


def shards(n_row, n_col, t_slab, w_cycle):
    _, panels, share, panel_width = t_slab.shape
    depth, jb = w_cycle.shape
    kc, rows, chips = panels * panel_width, n_col * share, n_row // CORES
    hbm = pl.BlockSpec(memory_space=pltpu.HBM)
    vmem = pl.BlockSpec(memory_space=pltpu.VMEM)
    dma = pltpu.SemaphoreType.DMA
    t_all, w_all = pl.pallas_call(
        functools.partial(gather_kernel, n_row, n_col),
        out_shape=(
            pltpu.VMEM((n_col, share, kc), t_slab.dtype),
            pltpu.VMEM((n_row, depth, jb), w_cycle.dtype),
        ),
        in_specs=[hbm] * 2,
        out_specs=(vmem, vmem),
        scratch_shapes=[
            pltpu.VMEM(t_slab.shape, t_slab.dtype),
            dma((2,)),
            dma((chips, PIECES)), dma((chips, PIECES)),
            dma((chips, PIECES)), dma((chips, PIECES)),
            dma((n_col,)), dma((n_col,)),
        ],
        compiler_params=pltpu.CompilerParams(
            collective_id=0, has_side_effects=True
        ),
        name="gather",
    )(t_slab, w_cycle)
    amp, z = pl.pallas_call(
        product_kernel,
        out_shape=(
            jax.ShapeDtypeStruct((kc // n_col, rows), t_slab.dtype),
            jax.ShapeDtypeStruct((rows, jb), jnp.float32),
        ),
        in_specs=[vmem] * 2,
        out_specs=(hbm, hbm),
        scratch_shapes=[
            pltpu.VMEM((jb // TILE, rows, TILE), jnp.float32),
            pltpu.VMEM((n_col, kc // n_col, rows), jnp.float32),
            pltpu.VMEM((kc // n_col, rows), t_slab.dtype),
            dma((jb // TILE,)),
            dma,
        ],
        compiler_params=pltpu.CompilerParams(vmem_limit_bytes=32 * 2**20),
        name="product",
    )(t_all, w_all)
    return amp.T, z


def solution(mesh):
    placed = (P("row", None, "col", None), P("row", "col"))
    return jax.shard_map(
        functools.partial(shards, mesh.shape["row"], mesh.shape["col"]),
        mesh=mesh,
        in_specs=placed,
        out_specs=(P("row", "col"), P("row", "col")),
        check_vma=False,
    )
```

```python
import functools

import jax
import jax.numpy as jnp
from jax import lax
from jax.experimental import pallas as pl
from jax.experimental.pallas import tpu as pltpu
from jax.sharding import PartitionSpec as P

CUTS = (0, 5, 8)
PIECES = len(CUTS) - 1
TILE = 256
CORES = 2


def gather_kernel(
    n_row, n_col, t_ref, w_ref, t_all, w_all, t_in, local_sem,
    chip_send, chip_recv, core_send, core_recv, t_send, t_recv,
):
    row, col = lax.axis_index("row"), lax.axis_index("col")
    chips, core = n_row // CORES, lax.rem(row, CORES)
    chip = row // CORES
    pieces = chip_send.shape[1]
    kc = t_all.shape[2]
    unit = w_ref.shape[1] // CUTS[-1]

    barrier = pltpu.get_barrier_semaphore()
    for k in range(1, n_col):
        pl.semaphore_signal(
            barrier, inc=1, device_id={"row": row, "col": lax.rem(col + k, n_col)}
        )
    for k in range(1, chips):
        pl.semaphore_signal(
            barrier, inc=1,
            device_id={"row": lax.rem(row + k * CORES, n_row), "col": col},
        )
    pl.semaphore_signal(
        barrier, inc=1, device_id={"row": chip * CORES + 1 - core, "col": col}
    )
    t_stage = pltpu.make_async_copy(t_ref, t_in, local_sem.at[0])
    t_stage.start()
    w_stage = pltpu.make_async_copy(w_ref, w_all.at[row], local_sem.at[1])
    w_stage.start()

    def chip_at(k):
        return lax.rem(chip + k + chips, chips)

    def columns(j):
        return pl.ds(CUTS[j] * unit, (CUTS[j + 1] - CUTS[j]) * unit)

    def to_chip(k, j):
        return pltpu.make_async_remote_copy(
            src_ref=w_all.at[row, :, columns(j)],
            dst_ref=w_all.at[row, :, columns(j)],
            send_sem=chip_send.at[k, j],
            recv_sem=chip_recv.at[k, j],
            device_id={"row": chip_at(k) * CORES + core, "col": col},
        )

    def to_core(k, j):
        slot = chip_at(-k) * CORES + core
        return pltpu.make_async_remote_copy(
            src_ref=w_all.at[slot, :, columns(j)],
            dst_ref=w_all.at[slot, :, columns(j)],
            send_sem=core_send.at[k, j],
            recv_sem=core_recv.at[k, j],
            device_id={"row": chip * CORES + 1 - core, "col": col},
        )

    def t_to(k):
        return pltpu.make_async_remote_copy(
            src_ref=t_all.at[col],
            dst_ref=t_all.at[col],
            send_sem=t_send.at[k],
            recv_sem=t_recv.at[k],
            device_id={"row": row, "col": lax.rem(col + k, n_col)},
        )

    others = range(1, chips)
    pl.semaphore_wait(barrier, chips + n_col - 1)
    w_stage.wait()
    for j in range(pieces):
        to_core(0, j).start()
    for j in range(pieces):
        for k in others:
            to_chip(k, j).start()
    t_stage.wait()
    t_all[col] = jnp.concatenate(
        [t_in[0, k] for k in range(t_in.shape[1])], axis=1
    )
    for k in range(1, n_col):
        t_to(k).start()

    for j in range(pieces):
        for k in others:
            to_chip(k, j).wait_recv()
            to_core(k, j).start()
    for k in range(1, n_col):
        t_to(k).wait_recv()
    for j in range(pieces):
        to_core(0, j).wait_recv()
        for k in others:
            to_core(k, j).wait_recv()

    for k in range(1, n_col):
        t_to(k).wait_send()
    for j in range(pieces):
        to_core(0, j).wait_send()
        for k in others:
            to_chip(k, j).wait_send()
            to_core(k, j).wait_send()


def product_kernel(t_ref, w_ref, amp_ref, z_ref, z_tiles, turned, amp_own, sems, amp_sem):
    col = lax.axis_index("col")
    tile = z_tiles.shape[2]
    kc = t_ref.shape[2]
    t_full = t_ref[...].reshape(-1, kc)
    copies = []
    for j in range(z_tiles.shape[0]):
        columns = pl.ds(j * tile, tile)
        z_tiles[j] = jnp.dot(
            t_full,
            w_ref[:, :, columns].reshape(kc, tile),
            preferred_element_type=jnp.float32,
        )
        copy = pltpu.make_async_copy(
            z_tiles.at[j], z_ref.at[:, columns], sems.at[j]
        )
        copy.start()
        copies.append(copy)
    turned[...] = t_full.astype(jnp.float32).T.reshape(turned.shape)
    amp_own[...] = turned[col].astype(amp_own.dtype)
    copy = pltpu.make_async_copy(amp_own, amp_ref, amp_sem)
    copy.start()
    copies.append(copy)
    for copy in copies:
        copy.wait()


def shards(n_row, n_col, t_slab, w_cycle):
    _, panels, share, panel_width = t_slab.shape
    depth, jb = w_cycle.shape
    kc, rows, chips = panels * panel_width, n_col * share, n_row // CORES
    hbm = pl.BlockSpec(memory_space=pltpu.HBM)
    vmem = pl.BlockSpec(memory_space=pltpu.VMEM)
    dma = pltpu.SemaphoreType.DMA
    t_all, w_all = pl.pallas_call(
        functools.partial(gather_kernel, n_row, n_col),
        out_shape=(
            pltpu.VMEM((n_col, share, kc), t_slab.dtype),
            pltpu.VMEM((n_row, depth, jb), w_cycle.dtype),
        ),
        in_specs=[hbm] * 2,
        out_specs=(vmem, vmem),
        scratch_shapes=[
            pltpu.VMEM(t_slab.shape, t_slab.dtype),
            dma((2,)),
            dma((chips, PIECES)), dma((chips, PIECES)),
            dma((chips, PIECES)), dma((chips, PIECES)),
            dma((n_col,)), dma((n_col,)),
        ],
        compiler_params=pltpu.CompilerParams(
            collective_id=0, has_side_effects=True
        ),
        name="gather",
    )(t_slab, w_cycle)
    amp, z = pl.pallas_call(
        product_kernel,
        out_shape=(
            jax.ShapeDtypeStruct((kc // n_col, rows), t_slab.dtype),
            jax.ShapeDtypeStruct((rows, jb), jnp.float32),
        ),
        in_specs=[vmem] * 2,
        out_specs=(hbm, hbm),
        scratch_shapes=[
            pltpu.VMEM((jb // TILE, rows, TILE), jnp.float32),
            pltpu.VMEM((n_col, kc // n_col, rows), jnp.float32),
            pltpu.VMEM((kc // n_col, rows), t_slab.dtype),
            dma((jb // TILE,)),
            dma,
        ],
        compiler_params=pltpu.CompilerParams(vmem_limit_bytes=32 * 2**20),
        name="product",
    )(t_all, w_all)
    return amp.T, z


def solution(mesh):
    placed = (P("row", None, "col", None), P("row", "col"))
    return jax.shard_map(
        functools.partial(shards, mesh.shape["row"], mesh.shape["col"]),
        mesh=mesh,
        in_specs=placed,
        out_specs=(P("row", "col"), P("row", "col")),
        check_vma=False,
    )
```

```python
import functools

import jax
import jax.numpy as jnp
from jax import lax
from jax.experimental import pallas as pl
from jax.experimental.pallas import tpu as pltpu
from jax.sharding import PartitionSpec as P

CUTS = (0, 8)
PIECES = len(CUTS) - 1
TILE = 256
CORES = 2


def gather_kernel(
    n_row, n_col, t_ref, w_ref, t_all, w_all, t_in, local_sem,
    chip_send, chip_recv, core_send, core_recv, t_send, t_recv,
):
    row, col = lax.axis_index("row"), lax.axis_index("col")
    chips, core = n_row // CORES, lax.rem(row, CORES)
    chip = row // CORES
    pieces = chip_send.shape[1]
    kc = t_all.shape[2]
    unit = w_ref.shape[1] // CUTS[-1]

    barrier = pltpu.get_barrier_semaphore()
    for k in range(1, n_col):
        pl.semaphore_signal(
            barrier, inc=1, device_id={"row": row, "col": lax.rem(col + k, n_col)}
        )
    for k in range(1, chips):
        pl.semaphore_signal(
            barrier, inc=1,
            device_id={"row": lax.rem(row + k * CORES, n_row), "col": col},
        )
    pl.semaphore_signal(
        barrier, inc=1, device_id={"row": chip * CORES + 1 - core, "col": col}
    )
    t_stage = pltpu.make_async_copy(t_ref, t_in, local_sem.at[0])
    t_stage.start()
    w_stage = pltpu.make_async_copy(w_ref, w_all.at[row], local_sem.at[1])
    w_stage.start()

    def chip_at(k):
        return lax.rem(chip + k + chips, chips)

    def columns(j):
        return pl.ds(CUTS[j] * unit, (CUTS[j + 1] - CUTS[j]) * unit)

    def to_chip(k, j):
        return pltpu.make_async_remote_copy(
            src_ref=w_all.at[row, :, columns(j)],
            dst_ref=w_all.at[row, :, columns(j)],
            send_sem=chip_send.at[k, j],
            recv_sem=chip_recv.at[k, j],
            device_id={"row": chip_at(k) * CORES + core, "col": col},
        )

    def to_core(k, j):
        slot = chip_at(-k) * CORES + core
        return pltpu.make_async_remote_copy(
            src_ref=w_all.at[slot, :, columns(j)],
            dst_ref=w_all.at[slot, :, columns(j)],
            send_sem=core_send.at[k, j],
            recv_sem=core_recv.at[k, j],
            device_id={"row": chip * CORES + 1 - core, "col": col},
        )

    def t_to(k):
        return pltpu.make_async_remote_copy(
            src_ref=t_all.at[col],
            dst_ref=t_all.at[col],
            send_sem=t_send.at[k],
            recv_sem=t_recv.at[k],
            device_id={"row": row, "col": lax.rem(col + k, n_col)},
        )

    others = range(1, chips)
    pl.semaphore_wait(barrier, chips + n_col - 1)
    w_stage.wait()
    for j in range(pieces):
        to_core(0, j).start()
    for j in range(pieces):
        for k in others:
            to_chip(k, j).start()
    t_stage.wait()
    t_all[col] = jnp.concatenate(
        [t_in[0, k] for k in range(t_in.shape[1])], axis=1
    )
    for k in range(1, n_col):
        t_to(k).start()

    for j in range(pieces):
        for k in others:
            to_chip(k, j).wait_recv()
            to_core(k, j).start()
    for k in range(1, n_col):
        t_to(k).wait_recv()
    for j in range(pieces):
        to_core(0, j).wait_recv()
        for k in others:
            to_core(k, j).wait_recv()

    for k in range(1, n_col):
        t_to(k).wait_send()
    for j in range(pieces):
        to_core(0, j).wait_send()
        for k in others:
            to_chip(k, j).wait_send()
            to_core(k, j).wait_send()


def product_kernel(t_ref, w_ref, amp_ref, z_ref, z_tiles, turned, amp_own, sems, amp_sem):
    col = lax.axis_index("col")
    tile = z_tiles.shape[2]
    kc = t_ref.shape[2]
    t_full = t_ref[...].reshape(-1, kc)
    copies = []
    for j in range(z_tiles.shape[0]):
        columns = pl.ds(j * tile, tile)
        z_tiles[j] = jnp.dot(
            t_full,
            w_ref[:, :, columns].reshape(kc, tile),
            preferred_element_type=jnp.float32,
        )
        copy = pltpu.make_async_copy(
            z_tiles.at[j], z_ref.at[:, columns], sems.at[j]
        )
        copy.start()
        copies.append(copy)
    turned[...] = t_full.astype(jnp.float32).T.reshape(turned.shape)
    amp_own[...] = turned[col].astype(amp_own.dtype)
    copy = pltpu.make_async_copy(amp_own, amp_ref, amp_sem)
    copy.start()
    copies.append(copy)
    for copy in copies:
        copy.wait()


def shards(n_row, n_col, t_slab, w_cycle):
    _, panels, share, panel_width = t_slab.shape
    depth, jb = w_cycle.shape
    kc, rows, chips = panels * panel_width, n_col * share, n_row // CORES
    hbm = pl.BlockSpec(memory_space=pltpu.HBM)
    vmem = pl.BlockSpec(memory_space=pltpu.VMEM)
    dma = pltpu.SemaphoreType.DMA
    t_all, w_all = pl.pallas_call(
        functools.partial(gather_kernel, n_row, n_col),
        out_shape=(
            pltpu.VMEM((n_col, share, kc), t_slab.dtype),
            pltpu.VMEM((n_row, depth, jb), w_cycle.dtype),
        ),
        in_specs=[hbm] * 2,
        out_specs=(vmem, vmem),
        scratch_shapes=[
            pltpu.VMEM(t_slab.shape, t_slab.dtype),
            dma((2,)),
            dma((chips, PIECES)), dma((chips, PIECES)),
            dma((chips, PIECES)), dma((chips, PIECES)),
            dma((n_col,)), dma((n_col,)),
        ],
        compiler_params=pltpu.CompilerParams(
            collective_id=0, has_side_effects=True
        ),
        name="gather",
    )(t_slab, w_cycle)
    amp, z = pl.pallas_call(
        product_kernel,
        out_shape=(
            jax.ShapeDtypeStruct((kc // n_col, rows), t_slab.dtype),
            jax.ShapeDtypeStruct((rows, jb), jnp.float32),
        ),
        in_specs=[vmem] * 2,
        out_specs=(hbm, hbm),
        scratch_shapes=[
            pltpu.VMEM((jb // TILE, rows, TILE), jnp.float32),
            pltpu.VMEM((n_col, kc // n_col, rows), jnp.float32),
            pltpu.VMEM((kc // n_col, rows), t_slab.dtype),
            dma((jb // TILE,)),
            dma,
        ],
        compiler_params=pltpu.CompilerParams(vmem_limit_bytes=32 * 2**20),
        name="product",
    )(t_all, w_all)
    return amp.T, z


def solution(mesh):
    placed = (P("row", None, "col", None), P("row", "col"))
    return jax.shard_map(
        functools.partial(shards, mesh.shape["row"], mesh.shape["col"]),
        mesh=mesh,
        in_specs=placed,
        out_specs=(P("row", "col"), P("row", "col")),
        check_vma=False,
    )
```
